256 devices in a mesh: sample: 4 (over z_lo, core), row: 16 (over y, z_hi), col: 4 (over x).
Axes of the slice: x: 4, y: 4, z: 8 (z_hi: 4, z_lo: 2; z = z_hi * 2 + z_lo), core: 2. Of those that a mesh axis runs over, the one named last changes fastest.
Arguments:
- single: bfloat16 [16384, 384], P(('sample', 'row')), parts along dimension 0, may hold values from -16 to 16
- pair_bias: bfloat16 [64, 4096, 4096], P('sample', 'row', 'col'), parts along dimension 0, may hold values from -4 to 400
- token_mask: int32 [16384], P('sample'), parts along dimension 0, may hold values from 0 to 1, as said below
- norm_gain: float32 [384], replicated, may hold values from 0.25 to 1.75
- w_query: bfloat16 [384, 384], replicated, may hold values from -0.3125 to 0.3125
- query_bias: float32 [384], replicated, may hold values from -3 to 3
- w_key: bfloat16 [384, 384], replicated, may hold values from -0.3125 to 0.3125
- w_value: bfloat16 [384, 384], replicated, may hold values from -0.3125 to 0.3125
- w_gate: bfloat16 [384, 384], replicated, may hold values from -0.3125 to 0.3125
- w_out: bfloat16 [384, 384], P(None, 'col'), may hold values from -0.3125 to 0.3125
Outputs:
- updated: float32 [16384, 384], P(('sample', 'row'), 'col'), parts along dimension 0
The draws below stay inside these ranges and needn't reach their ends.
There are 4 independent parts, one for each index of `sample`. The reference program is written for one: setup_inputs(seed, part) draws one part's arguments, and reference() takes and returns one part's arrays. A program takes and returns all parts, laid end to end along the dimension named above; an argument that names none is the same for every part. Nothing has to cross between parts.
Inputs may be any that keep to these rules, and one draw needn't show every extreme that they name: `token_mask`: 1 for a leading run of 512 or more tokens and 0 for every token after it.
All inputs are finite; a program needn't handle non-finite values.
Results may differ from the reference program's by a relative error of at most 0.0014.
Values may be sent and summed in bfloat16 or wider, within the bound.
A program may use at most 128 MiB of HBM per device.

```python
import math
import jax
import jax.numpy as jnp
from jax import lax

D = 384
HEADS = 16
TOKENS = 4096


def draw_single(key, part):
    result = jnp.clip(jax.random.normal(key, (TOKENS, D), jnp.float32), -4.0, 4.0)
    return result.astype(jnp.bfloat16)


def draw_pair_bias(key, part):
    shape = (HEADS, TOKENS, TOKENS)
    result = jnp.clip(jax.random.normal(key, shape, jnp.float32), -4.0, 4.0)
    return result.astype(jnp.bfloat16)


def draw_token_mask(key, part):
    length = jax.random.randint(key, (), TOKENS // 8, TOKENS)
    return (jnp.arange(TOKENS, dtype=jnp.int32) < length).astype(jnp.int32)


def level_of(own_key, extent, pieces, low, largest):
    def one(position, shards_of):
        steps = jax.random.uniform(jax.random.fold_in(jax.random.fold_in(own_key, 6), position), (shards_of,), jnp.float32, low / len(pieces), largest / len(pieces))
        return jnp.repeat(jnp.exp(steps), extent[position] // shards_of).reshape((-1,) + (1,) * (len(extent) - position - 1))

    loudness = one(*pieces[0])
    for cut in pieces[1:]:
        loudness = loudness * one(*cut)
    return loudness


def bell_draw(key, dims, deviation, reach, cuts=(), kind=jnp.bfloat16):
    loudness = level_of(key, dims, cuts, -0.22, 0.18) if cuts else 1.0
    array = jax.random.normal(key, dims, jnp.float32) * deviation * loudness
    return jnp.minimum(jnp.maximum(array, -reach), reach).astype(kind)


def setup_inputs(seed: int = 0, part: int = 0) -> dict:
    key_of = jax.random.split(jax.random.key(seed), 11)
    own_keys = jax.random.split(jax.random.fold_in(key_of[10], part), 11)
    single = draw_single(jax.random.fold_in(jax.random.fold_in(key_of[10], part), 71), part)
    pair_bias = draw_pair_bias(jax.random.fold_in(jax.random.fold_in(key_of[10], part), 71), part)
    token_mask = draw_token_mask(jax.random.fold_in(jax.random.fold_in(key_of[10], part), 71), part)
    norm_gain = jnp.clip(1.0 + 0.15 * jax.random.normal(key_of[3], (D,), jnp.float32), 0.25, 1.75)
    w_query = bell_draw(key_of[4], (D, D), D ** -0.5, 0.3125)
    query_bias = bell_draw(key_of[5], (D,), 0.5, 3.0, (), jnp.float32)
    w_key = bell_draw(key_of[6], (D, D), D ** -0.5, 0.3125)
    w_value = bell_draw(key_of[7], (D, D), D ** -0.5, 0.3125)
    w_gate = bell_draw(key_of[8], (D, D), D ** -0.5, 0.3125)
    w_out = bell_draw(key_of[9], (D, D), D ** -0.5, 0.3125, ((1, 4),))
    return {"single": single, "pair_bias": pair_bias, "token_mask": token_mask, "norm_gain": norm_gain, "w_query": w_query, "query_bias": query_bias, "w_key": w_key, "w_value": w_value, "w_gate": w_gate, "w_out": w_out}


def layer_norm(single, norm_gain):
    values_f32 = single.astype(jnp.float32)
    row_mean = lax.optimization_barrier(jnp.mean(values_f32, axis=1, keepdims=True))
    centered = values_f32 - row_mean
    row_var = lax.optimization_barrier(jnp.mean(centered * centered, axis=1, keepdims=True))
    return (centered * lax.rsqrt(row_var + 1e-05) * norm_gain).astype(jnp.bfloat16)

def reference(single, pair_bias, token_mask, norm_gain, w_query, query_bias, w_key, w_value, w_gate, w_out):
    head_dim = D // HEADS
    inv_sqrt = 1.0 / math.sqrt(head_dim)
    normed = layer_norm(single, norm_gain)
    query = ((jnp.dot(normed, w_query, preferred_element_type=jnp.float32) + query_bias) * inv_sqrt).astype(jnp.bfloat16)
    key_rows = jnp.dot(normed, w_key, preferred_element_type=jnp.float32).astype(jnp.bfloat16)
    value_rows = jnp.dot(normed, w_value, preferred_element_type=jnp.float32).astype(jnp.bfloat16)
    gate_act = jax.nn.sigmoid(jnp.dot(normed, w_gate, preferred_element_type=jnp.float32))
    mask_term = (token_mask.astype(jnp.float32) - 1.0) * 1000000.0
    query_heads = query.reshape(TOKENS, HEADS, head_dim).transpose(1, 0, 2)
    key_heads = key_rows.reshape(TOKENS, HEADS, head_dim).transpose(1, 0, 2)
    value_heads = value_rows.reshape(TOKENS, HEADS, head_dim).transpose(1, 0, 2)

    def one_head(packed):
        query_h, key_h, value_h, bias_h = packed
        logits = jnp.dot(query_h, key_h.T, preferred_element_type=jnp.float32)
        logits = logits + bias_h.astype(jnp.float32) + mask_term[None, :]
        row_peak = lax.optimization_barrier(jnp.max(logits, axis=1, keepdims=True))
        exp_scores = jnp.exp(logits - row_peak)
        row_total = lax.optimization_barrier(jnp.sum(exp_scores, axis=1, keepdims=True))
        weighted = jnp.dot(exp_scores.astype(jnp.bfloat16), value_h, preferred_element_type=jnp.float32)
        return weighted / row_total
    attended = lax.map(one_head, (query_heads, key_heads, value_heads, pair_bias))
    attended = attended.transpose(1, 0, 2).reshape(TOKENS, D)
    gated = (gate_act * attended).astype(jnp.bfloat16)
    return single.astype(jnp.float32) + jnp.dot(gated, w_out, preferred_element_type=jnp.float32)
```

```python
import functools
import math

import jax
import jax.numpy as jnp
from jax import lax
from jax.experimental import pallas as pl
from jax.experimental.pallas import tpu as pltpu
from jax.sharding import PartitionSpec as P

D = 384
HEADS = 16
HD = 24
PAD = 32
WIDE = HEADS * PAD
GROUPS = 4
LANES = 128
ROWS = 256
PART = 64
OUTW = 96
MESH = pl.DeviceIdType.MESH
F32 = jnp.float32
BF16 = jnp.bfloat16
MASK_HI = 999424.0
MASK_LO = 576.0


def iota(shape, dim):
    return lax.broadcasted_iota(jnp.int32, shape, dim)


def mm(a, b):
    return lax.dot_general(a, b, (((1,), (0,)), ((), ())), preferred_element_type=F32)


def mm_nt(a, b):
    return lax.dot_general(a, b, (((1,), (1,)), ((), ())), preferred_element_type=F32)


def layer_norm(values, gain):
    values = values.astype(F32)
    centered = values - jnp.mean(values, axis=1, keepdims=True)
    var = jnp.mean(centered * centered, axis=1, keepdims=True)
    return (centered * lax.rsqrt(var + 1e-05) * gain).astype(BF16)


def spread_matrix(first):
    def make(width):
        src, dst = iota((D, width), 0), iota((D, width), 1)
        hit = (src == (dst // PAD + first) * HD + dst % PAD) & (dst % PAD < HD)
        return jnp.where(hit, 1.0, 0.0).astype(BF16)

    return make


def kernel(
    single, bias, mask, gain, w_query, q_bias, w_key, w_value, w_gate, w_out, out,
    s_v, b_v, mask_v, gain_v, qb_v, wq_v, wk_v, wv_v, wg_v, wo_v,
    ybuf, kbuf, qm, wkt, wvp, wop, gate_v, cols_v, kt, vm, p4, mrun, acc, part, got, gbuf,
    lsem, bsem, zs, zr, ys, yr, xs, xr, ps, pr, gs, gr,
):
    col = lax.axis_index("col")
    row = lax.axis_index("row")
    x, y, z = col, row // 4, row % 4

    def dev(cx, cy, cz):
        return {"row": cy * 4 + cz, "col": cx}

    def rdma(src, dst, ssem, rsem, target):
        return pltpu.make_async_remote_copy(
            src_ref=src, dst_ref=dst, send_sem=ssem, recv_sem=rsem,
            device_id=target, device_id_type=MESH,
        )

    tokens = 4 * ROWS
    loads = [
        (single, s_v), (gain, gain_v), (q_bias, qb_v), (w_query, wq_v), (w_key, wk_v),
        (w_value, wv_v), (w_gate, wg_v), (w_out, wo_v),
        (mask.at[pl.ds(pl.multiple_of(col * tokens, tokens), tokens)], mask_v),
    ]
    loads = [pltpu.make_async_copy(a, b, lsem.at[i]) for i, (a, b) in enumerate(loads)]
    for load in loads:
        load.start()

    def chunk_cols(d):
        return pl.ds(pl.multiple_of(((z + d) % 4) * ROWS, ROWS), ROWS)

    order = (0, 1, 3, 2)

    def bias_load(d):
        return pltpu.make_async_copy(bias.at[:, :, chunk_cols(d)], b_v.at[d], bsem.at[d])

    barrier = pltpu.get_barrier_semaphore()
    peers = [dev((x + k) % 4, y, z) for k in (1, 2, 3)]
    peers += [dev(x, (y + k) % 4, z) for k in (1, 2, 3)]
    peers += [dev(x, y, (z + k) % 4) for k in (1, 2, 3)]
    for peer in peers:
        pl.semaphore_signal(barrier, inc=1, device_id=peer, device_id_type=MESH)
    for d in order:
        bias_load(d).start()

    for load in loads:
        load.wait()
    pl.semaphore_wait(barrier, len(peers))

    diag = x == y
    mine = pl.ds(pl.multiple_of(x * PART, PART), PART)
    own = s_v.at[mine]

    def zc(d):
        return rdma(own, ybuf.at[y, d], zs.at[d], zr.at[d], dev(x, y, (z + 4 - d) % 4))

    def yc(d, k):
        return rdma(ybuf.at[y, d], ybuf.at[y, d], ys.at[d, k], yr.at[d, 4 - k], dev(x, (y + k) % 4, z))

    def yw(d, k):
        other = (y + k) % 4
        return rdma(ybuf.at[other, d], ybuf.at[other, d], ys.at[d, k], yr.at[d, k], dev(x, other, z))

    def xc(d, k):
        other = (x + k) % 4
        return rdma(ybuf.at[other, d], kbuf.at[d, mine], xs.at[d, k], xr.at[d, 4 - k], dev(other, y, z))

    def xw(d, k):
        other = (x + k) % 4
        where = kbuf.at[d, pl.ds(pl.multiple_of(other * PART, PART), PART)]
        return rdma(where, where, xs.at[d, k], xr.at[d, k], dev(other, y, z))

    def direct(k):
        return rdma(s_v, kbuf.at[0], ys.at[0, k], xr.at[0, 0], dev(x, (y + k) % 4, z))

    def y_send(d):
        zc(d).wait_recv()
        for k in (1, 3, 2):
            yc(d, k).start()

    def x_send(d):
        for k in (1, 3, 2):
            yw(d, k).wait_recv()
        for k in (1, 3, 2):
            xc(d, k).start()

    def x_wait(d):
        for k in (1, 3, 2):
            xw(d, k).wait_recv()
        kbuf[d, mine] = ybuf[x, d]

    for d in (1, 3, 2):
        zc(d).start()

    @pl.when(diag)
    def _():
        for k in (1, 3, 2):
            direct(k).start()
        kbuf[0] = s_v[...]

    gain_row = gain_v[...].reshape(1, D)
    normed = layer_norm(s_v[...], gain_row)
    spread = spread_matrix(0)(WIDE)
    dst, src = iota((WIDE, D), 0), iota((WIDE, D), 1)
    hit = (src == (dst // PAD) * HD + dst % PAD) & (dst % PAD < HD)
    spread_t = jnp.where(hit, 1.0, 0.0).astype(BF16)
    wkt[...] = mm_nt(spread_t, wk_v[...]).astype(BF16)
    wvp[...] = mm(wv_v[...], spread).astype(BF16)
    wqp = mm(wq_v[...], spread).astype(BF16)
    qb_row = qb_v[...].reshape(1, D)
    qb_hi = qb_row.astype(BF16)
    qb_rest = qb_row - qb_hi.astype(F32)
    qb_mid = qb_rest.astype(BF16)
    qb_lo = (qb_rest - qb_mid.astype(F32)).astype(BF16)
    qb_pad = mm(qb_hi, spread) + mm(qb_mid, spread) + mm(qb_lo, spread)
    query = (mm(normed, wqp) + qb_pad) * (1.0 / math.sqrt(HD))
    wide_lane = iota((ROWS, WIDE), 1) % PAD
    query = jnp.where((wide_lane == HD) | (wide_lane == HD + 1), 1.0, query)
    lane = iota((ROWS, LANES), 1)
    head_of = lane // PAD
    for h in range(HEADS):
        g, hh = divmod(h, 4)
        qm[h] = jnp.where(head_of == hh, query[:, g * LANES : (g + 1) * LANES], 0.0).astype(BF16)

    y_send(1)
    y_send(3)

    wop[...] = mm(spread_t, wo_v[...]).astype(BF16)
    wg = mm(wg_v[...], spread_matrix(col * 4)(LANES)).astype(BF16)
    gate_v[...] = jax.nn.sigmoid(mm(normed, wg))
    pick = (iota((D, OUTW), 0) == iota((D, OUTW), 1) + col * OUTW)
    cols_v[...] = mm(s_v[...], jnp.where(pick, 1.0, 0.0).astype(BF16))
    mrun[...] = jnp.full(mrun.shape, -1e30, F32)
    acc[...] = jnp.zeros(acc.shape, F32)

    y_send(2)
    x_send(1)

    @pl.when(jnp.logical_not(diag))
    def _():
        direct(1).wait_recv()

    def prepare(d):
        normed_k = layer_norm(kbuf[d], gain_row)
        keys = mm_nt(wkt[...], normed_k)
        flags = mask_v[chunk_cols(d)].reshape(1, ROWS).astype(F32) - 1.0
        feature = iota((WIDE, ROWS), 0) % PAD
        term = jnp.where(feature == HD, MASK_HI, jnp.where(feature == HD + 1, MASK_LO, 0.0))
        kt[...] = (keys + term * flags).astype(BF16)
        value = mm(normed_k, wvp[...])
        value = jnp.where(wide_lane == HD, 1.0, value)
        for h in range(HEADS):
            g, hh = divmod(h, 4)
            vm[g, hh * ROWS : (hh + 1) * ROWS] = jnp.where(
                head_of == hh, value[:, g * LANES : (g + 1) * LANES], 0.0
            ).astype(BF16)

    def group(d, g):
        key_tile = kt[pl.ds(pl.multiple_of(g * LANES, LANES), LANES)]
        old = mrun[g]
        new = old
        for hh in range(4):
            logits = mm(qm[g * 4 + hh], key_tile) + b_v[d, g * 4 + hh].astype(F32)
            peak = jnp.maximum(jnp.max(logits, axis=1, keepdims=True), old[:, hh * PAD : hh * PAD + 1])
            p4[:, hh * ROWS : (hh + 1) * ROWS] = jnp.exp(logits - peak).astype(BF16)
            new = jnp.where(head_of == hh, peak, new)
        total = acc[g] * jnp.exp(old - new) + mm(p4[...], vm[g])
        return total, new

    def run_group(d, g):
        total, new = group(d, g)
        acc[g] = total
        mrun[g] = new

    def chunk(d):
        bias_load(d).wait()
        prepare(d)

        def body(g, carry):
            run_group(d, g)
            return carry

        lax.fori_loop(0, GROUPS, body, 0)

    chunk(0)
    x_send(3)
    x_send(2)
    x_wait(1)
    chunk(1)
    x_wait(3)
    chunk(3)
    x_wait(2)
    bias_load(2).wait()
    prepare(2)

    sub = lane % PAD

    def finish(g):
        total, new = group(2, g)
        high = new.astype(BF16).astype(F32)
        low = (new - high).astype(BF16).astype(F32)
        total = total * jnp.exp(new - (high + low))
        return jnp.where(sub == HD + 1, high, jnp.where(sub == HD + 2, low, total))

    def pc(k):
        other = (x + k) % 4
        return rdma(part.at[other], got.at[4 - k], ps.at[k], pr.at[4 - k], dev(other, y, z))

    def pw(k):
        other = (x + k) % 4
        return rdma(got.at[k], got.at[k], ps.at[k], pr.at[k], dev(other, y, z))

    def send_body(k, carry):
        g = (x + k) % 4
        part[g] = finish(g)
        pc(k).start()
        return carry

    lax.fori_loop(1, 4, send_body, 0)
    got[0] = finish(x)
    for k in (1, 2, 3):
        pw(k).wait_recv()

    a, b = iota((LANES, LANES), 0), iota((LANES, LANES), 1)
    same = a // PAD == b // PAD
    pick_peak = jnp.where(same & ((a % PAD == HD + 1) | (a % PAD == HD + 2)), 1.0, 0.0).astype(BF16)
    pick_total = jnp.where(same & (a % PAD == HD), 1.0, 0.0).astype(BF16)
    peaks = [mm(got[k].astype(BF16), pick_peak) for k in range(4)]
    peak = jnp.maximum(jnp.maximum(peaks[0], peaks[1]), jnp.maximum(peaks[2], peaks[3]))
    total = sum(got[k] * jnp.exp(peaks[k] - peak) for k in range(4))
    total_hi = total.astype(BF16)
    total_lo = (total - total_hi.astype(F32)).astype(BF16)
    denom = mm(total_hi, pick_total) + mm(total_lo, pick_total)
    gated = jnp.where(sub < HD, gate_v[...] * (total / denom), 0.0).astype(BF16)
    gbuf[x] = gated

    def gc(k):
        return rdma(gbuf.at[x], gbuf.at[x], gs.at[k], gr.at[4 - k], dev((x + k) % 4, y, z))

    def gw(k):
        other = (x + k) % 4
        return rdma(gbuf.at[other], gbuf.at[other], gs.at[k], gr.at[k], dev(other, y, z))

    for k in (1, 3, 2):
        gc(k).start()
    for k in (1, 3, 2):
        gw(k).wait_recv()
    result = cols_v[...]
    for g in range(GROUPS):
        result = result + mm(gbuf[g], wop[g * LANES : (g + 1) * LANES])
    out[...] = result

    for d in (1, 3, 2):
        zc(d).wait_send()
        for k in (1, 2, 3):
            yc(d, k).wait_send()
            xc(d, k).wait_send()

    @pl.when(diag)
    def _():
        for k in (1, 2, 3):
            direct(k).wait_send()

    for k in (1, 2, 3):
        pc(k).wait_send()
        gc(k).wait_send()


def on_device(*args):
    hbm = pl.BlockSpec(memory_space=pltpu.MemorySpace.HBM)
    sem = pltpu.SemaphoreType.DMA
    vmem = pltpu.VMEM
    return pl.pallas_call(
        kernel,
        name="attention",
        out_shape=jax.ShapeDtypeStruct((ROWS, OUTW), F32),
        in_specs=[hbm] * 10,
        out_specs=pl.BlockSpec(memory_space=pltpu.VMEM),
        scratch_shapes=[
            vmem((ROWS, D), BF16),
            vmem((4, HEADS, ROWS, ROWS), BF16),
            vmem((4 * ROWS,), jnp.int32),
            vmem((D,), F32),
            vmem((D,), F32),
            vmem((D, D), BF16),
            vmem((D, D), BF16),
            vmem((D, D), BF16),
            vmem((D, D), BF16),
            vmem((D, OUTW), BF16),
            vmem((4, 4, PART, D), BF16),
            vmem((4, ROWS, D), BF16),
            vmem((HEADS, ROWS, LANES), BF16),
            vmem((WIDE, D), BF16),
            vmem((D, WIDE), BF16),
            vmem((WIDE, OUTW), BF16),
            vmem((ROWS, LANES), F32),
            vmem((ROWS, OUTW), F32),
            vmem((WIDE, ROWS), BF16),
            vmem((GROUPS, 4 * ROWS, LANES), BF16),
            vmem((ROWS, 4 * ROWS), BF16),
            vmem((GROUPS, ROWS, LANES), F32),
            vmem((GROUPS, ROWS, LANES), F32),
            vmem((GROUPS, ROWS, LANES), F32),
            vmem((4, ROWS, LANES), F32),
            vmem((4, ROWS, LANES), BF16),
            sem((9,)), sem((4,)), sem((4,)), sem((4,)),
            sem((4, 4)), sem((4, 4)), sem((4, 4)), sem((4, 4)),
            sem((4,)), sem((4,)), sem((4,)), sem((4,)),
        ],
        compiler_params=pltpu.CompilerParams(
            collective_id=0, has_side_effects=True, vmem_limit_bytes=58 * 1024 * 1024
        ),
    )(*args)


def solution(mesh):
    return jax.shard_map(
        on_device,
        mesh=mesh,
        in_specs=(
            P(("sample", "row"), None),
            P("sample", "row", "col"),
            P("sample"),
            P(),
            P(),
            P(),
            P(),
            P(),
            P(),
            P(None, "col"),
        ),
        out_specs=P(("sample", "row"), "col"),
        check_vma=False,
    )
```

```python
import functools
import math

import jax
import jax.numpy as jnp
from jax import lax
from jax.experimental import pallas as pl
from jax.experimental.pallas import tpu as pltpu
from jax.sharding import PartitionSpec as P

D = 384
HEADS = 16
HD = 24
PAD = 32
WIDE = HEADS * PAD
GROUPS = 4
LANES = 128
ROWS = 256
PART = 64
OUTW = 96
MESH = pl.DeviceIdType.MESH
F32 = jnp.float32
BF16 = jnp.bfloat16
MASK_HI = 999424.0
MASK_LO = 576.0


def iota(shape, dim):
    return lax.broadcasted_iota(jnp.int32, shape, dim)


def mm(a, b):
    return lax.dot_general(a, b, (((1,), (0,)), ((), ())), preferred_element_type=F32)


def mm_nt(a, b):
    return lax.dot_general(a, b, (((1,), (1,)), ((), ())), preferred_element_type=F32)


def layer_norm(values, gain):
    values = values.astype(F32)
    centered = values - jnp.mean(values, axis=1, keepdims=True)
    var = jnp.mean(centered * centered, axis=1, keepdims=True)
    return (centered * lax.rsqrt(var + 1e-05) * gain).astype(BF16)


def spread_matrix(width):
    src, dst = iota((D, width), 0), iota((D, width), 1)
    hit = (src == (dst // PAD) * HD + dst % PAD) & (dst % PAD < HD)
    return jnp.where(hit, 1.0, 0.0).astype(BF16)


def spread_rows(width, first):
    dst, src = iota((width, D), 0), iota((width, D), 1)
    hit = (src == (dst // PAD + first) * HD + dst % PAD) & (dst % PAD < HD)
    return jnp.where(hit, 1.0, 0.0).astype(BF16)


def kernel(
    single, bias, mask, gain, w_query, q_bias, w_key, w_value, w_gate, w_out, out,
    s_v, b_v, mask_v, gain_v, qb_v, wq_v, wk_v, wv_v, wg_v, wo_v,
    ybuf, kbuf, qm, wkt, wvp, gate_v, cols_v, kt, vm, p4, mrep, mrun, acc, part, got, gbuf,
    lsem, bsem, zs, zr, ys, yr, xs, xr, ps, pr, gs, gr,
):
    col = lax.axis_index("col")
    row = lax.axis_index("row")
    x, y, z = col, row // 4, row % 4

    def dev(cx, cy, cz):
        return {"row": cy * 4 + cz, "col": cx}

    def rdma(src, dst, ssem, rsem, target):
        return pltpu.make_async_remote_copy(
            src_ref=src, dst_ref=dst, send_sem=ssem, recv_sem=rsem,
            device_id=target, device_id_type=MESH,
        )

    barrier = pltpu.get_barrier_semaphore()
    peers = [dev((x + k) % 4, y, z) for k in (1, 2, 3)]
    peers += [dev(x, (y + k) % 4, z) for k in (1, 2, 3)]
    peers += [dev(x, y, (z + k) % 4) for k in (1, 2, 3)]
    for peer in peers:
        pl.semaphore_signal(barrier, inc=1, device_id=peer, device_id_type=MESH)

    tokens = 4 * ROWS
    loads = [
        (single, s_v), (gain, gain_v), (q_bias, qb_v), (w_query, wq_v), (w_key, wk_v),
        (w_value, wv_v), (w_gate, wg_v), (w_out, wo_v),
        (mask.at[pl.ds(pl.multiple_of(col * tokens, tokens), tokens)], mask_v),
    ]
    loads = [pltpu.make_async_copy(a, b, lsem.at[i]) for i, (a, b) in enumerate(loads)]
    for load in loads:
        load.start()

    def chunk_cols(d):
        return pl.ds(pl.multiple_of(((z + d) % 4) * ROWS, ROWS), ROWS)

    order = (0, 1, 3, 2)

    def bias_load(d):
        return pltpu.make_async_copy(bias.at[:, :, chunk_cols(d)], b_v.at[d], bsem.at[d])

    pl.semaphore_wait(barrier, len(peers))

    diag = x == y
    mine = pl.ds(pl.multiple_of(x * PART, PART), PART)
    own = single.at[mine]

    def zc(d):
        return rdma(own, ybuf.at[y, d], zs.at[d], zr.at[d], dev(x, y, (z + 4 - d) % 4))

    def yc(d, k):
        return rdma(ybuf.at[y, d], ybuf.at[y, d], ys.at[d, k], yr.at[d, 4 - k], dev(x, (y + k) % 4, z))

    def yw(d, k):
        other = (y + k) % 4
        return rdma(ybuf.at[other, d], ybuf.at[other, d], ys.at[d, k], yr.at[d, k], dev(x, other, z))

    def xc(d, k):
        other = (x + k) % 4
        return rdma(ybuf.at[other, d], kbuf.at[d, mine], xs.at[d, k], xr.at[d, 4 - k], dev(other, y, z))

    def xw(d, k):
        other = (x + k) % 4
        where = kbuf.at[d, pl.ds(pl.multiple_of(other * PART, PART), PART)]
        return rdma(where, where, xs.at[d, k], xr.at[d, k], dev(other, y, z))

    def direct(k):
        return rdma(single, kbuf.at[0], ys.at[0, k], xr.at[0, 0], dev(x, (y + k) % 4, z))

    def y_send(d):
        zc(d).wait_recv()
        for k in (1, 3, 2):
            yc(d, k).start()

    def x_send(d):
        for k in (1, 3, 2):
            yw(d, k).wait_recv()
        for k in (1, 3, 2):
            xc(d, k).start()

    def x_wait(d):
        for k in (1, 3, 2):
            xw(d, k).wait_recv()
        kbuf[d, mine] = ybuf[x, d]

    for d in (1, 3, 2):
        zc(d).start()

    @pl.when(diag)
    def _():
        for k in (1, 3, 2):
            direct(k).start()

    for d in order:
        bias_load(d).start()
    for load in loads:
        load.wait()

    @pl.when(diag)
    def _():
        kbuf[0] = s_v[...]

    gain_row = gain_v[...].reshape(1, D)
    normed = layer_norm(s_v[...], gain_row)
    spread = spread_matrix(WIDE)
    spread_t = spread_rows(WIDE, 0)
    wqp = mm(wq_v[...], spread).astype(BF16)
    qb_row = qb_v[...].reshape(1, D)
    qb_hi = qb_row.astype(BF16)
    qb_rest = qb_row - qb_hi.astype(F32)
    qb_mid = qb_rest.astype(BF16)
    qb_lo = (qb_rest - qb_mid.astype(F32)).astype(BF16)
    qb_pad = mm(qb_hi, spread) + mm(qb_mid, spread) + mm(qb_lo, spread)
    query = (mm(normed, wqp) + qb_pad) * (1.0 / math.sqrt(HD))
    wide_lane = iota((ROWS, WIDE), 1) % PAD
    query = jnp.where((wide_lane == HD) | (wide_lane == HD + 1), 1.0, query)
    lane = iota((ROWS, LANES), 1)
    head_of, sub = lane // PAD, lane % PAD
    for h in range(HEADS):
        g, hh = divmod(h, 4)
        qm[h] = jnp.where(head_of == hh, query[:, g * LANES : (g + 1) * LANES], 0.0).astype(BF16)
    wkt[...] = mm_nt(spread_t, wk_v[...]).astype(BF16)
    wvp[...] = mm(wv_v[...], spread).astype(BF16)

    y_send(1)
    y_send(3)

    wgt = mm_nt(spread_rows(LANES, col * 4), wg_v[...]).astype(BF16)
    gate_v[...] = jax.nn.sigmoid(mm_nt(wgt, normed))
    pick = iota((OUTW, D), 1) == iota((OUTW, D), 0) + col * OUTW
    cols_v[...] = mm_nt(jnp.where(pick, 1.0, 0.0).astype(BF16), s_v[...])
    mrep[...] = jnp.full(mrep.shape, -1e30, F32)
    mrun[...] = jnp.full(mrun.shape, -1e30, F32)
    acc[...] = jnp.zeros(acc.shape, F32)

    y_send(2)
    x_send(1)

    @pl.when(jnp.logical_not(diag))
    def _():
        direct(1).wait_recv()

    def prepare(d):
        normed_k = layer_norm(kbuf[d], gain_row)
        keys = mm_nt(wkt[...], normed_k)
        flags = mask_v[chunk_cols(d)].reshape(1, ROWS).astype(F32) - 1.0
        feature = iota((WIDE, ROWS), 0) % PAD
        term = jnp.where(feature == HD, MASK_HI, jnp.where(feature == HD + 1, MASK_LO, 0.0))
        kt[...] = (keys + term * flags).astype(BF16)
        value = mm(normed_k, wvp[...])
        value = jnp.where(wide_lane == HD, 1.0, value)
        for h in range(HEADS):
            g, hh = divmod(h, 4)
            vm[g, hh * ROWS : (hh + 1) * ROWS] = jnp.where(
                head_of == hh, value[:, g * LANES : (g + 1) * LANES], 0.0
            ).astype(BF16)

    def group(d, g):
        key_tile = kt[pl.ds(pl.multiple_of(g * LANES, LANES), LANES)]
        old = mrun[g]
        new = old
        for hh in range(4):
            h = g * 4 + hh
            logits = mm(qm[h], key_tile) + b_v[d, h].astype(F32)
            peak = jnp.maximum(jnp.max(logits, axis=1, keepdims=True), mrep[h])
            mrep[h] = peak
            for j in (0, LANES):
                p4[:, hh * ROWS + j : hh * ROWS + j + LANES] = jnp.exp(logits[:, j : j + LANES] - peak).astype(BF16)
            new = jnp.where(head_of == hh, peak, new)
        total = acc[g] * jnp.exp(old - new) + mm(p4[...], vm[g])
        return total, new

    def run_group(d, g):
        acc[g], mrun[g] = group(d, g)

    def chunk(d):
        bias_load(d).wait()
        prepare(d)

        def body(g, carry):
            run_group(d, g)
            return carry

        lax.fori_loop(0, GROUPS, body, 0)

    chunk(0)
    x_send(3)
    x_send(2)
    x_wait(1)
    chunk(1)
    x_wait(3)
    chunk(3)
    x_wait(2)
    bias_load(2).wait()
    prepare(2)

    def pc(k):
        other = (x + k) % 4
        return rdma(part.at[other], got.at[4 - k], ps.at[k], pr.at[4 - k], dev(other, y, z))

    def pw(k):
        other = (x + k) % 4
        return rdma(got.at[k], got.at[k], ps.at[k], pr.at[k], dev(other, y, z))

    def finish(g):
        total, new = group(2, g)
        part[g] = jnp.where(sub == HD + 1, new, total).T

    def send_body(k, carry):
        finish((x + k) % 4)
        pc(k).start()
        return carry

    lax.fori_loop(1, 4, send_body, 0)
    finish(x)
    for k in (1, 2, 3):
        pw(k).wait_recv()

    rows = []
    for hh in range(4):
        parts = [part[x, hh * PAD : (hh + 1) * PAD]]
        parts += [got[k, hh * PAD : (hh + 1) * PAD] for k in (1, 2, 3)]
        peaks = [p[HD + 1 : HD + 2] for p in parts]
        peak = jnp.maximum(jnp.maximum(peaks[0], peaks[1]), jnp.maximum(peaks[2], peaks[3]))
        total = sum(p * jnp.exp(m - peak) for p, m in zip(parts, peaks))
        rows.append(gate_v[hh * PAD : hh * PAD + HD] * (total[0:HD] / total[HD : HD + 1]))
    gbuf[x] = jnp.concatenate(rows, axis=0).astype(BF16)

    def gc(k):
        return rdma(gbuf.at[x], gbuf.at[x], gs.at[k], gr.at[4 - k], dev((x + k) % 4, y, z))

    def gw(k):
        other = (x + k) % 4
        return rdma(gbuf.at[other], gbuf.at[other], gs.at[k], gr.at[k], dev(other, y, z))

    for k in (1, 3, 2):
        gc(k).start()
    for k in (1, 3, 2):
        gw(k).wait_recv()
    out[...] = cols_v[...] + mm(wo_v[...], gbuf[...].reshape(D, ROWS))

    for d in (1, 3, 2):
        zc(d).wait_send()
        for k in (1, 2, 3):
            yc(d, k).wait_send()
            xc(d, k).wait_send()

    @pl.when(diag)
    def _():
        for k in (1, 2, 3):
            direct(k).wait_send()

    for k in (1, 2, 3):
        pc(k).wait_send()
        gc(k).wait_send()


def on_device(*args):
    *rest, w_out = args
    hbm = pl.BlockSpec(memory_space=pltpu.MemorySpace.HBM)
    sem = pltpu.SemaphoreType.DMA
    vmem = pltpu.VMEM
    result = pl.pallas_call(
        kernel,
        name="attention",
        out_shape=jax.ShapeDtypeStruct((OUTW, ROWS), F32),
        in_specs=[hbm] * 10,
        out_specs=pl.BlockSpec(memory_space=pltpu.VMEM),
        scratch_shapes=[
            vmem((ROWS, D), BF16),
            vmem((4, HEADS, ROWS, ROWS), BF16),
            vmem((4 * ROWS,), jnp.int32),
            vmem((D,), F32),
            vmem((D,), F32),
            vmem((D, D), BF16),
            vmem((D, D), BF16),
            vmem((D, D), BF16),
            vmem((D, D), BF16),
            vmem((OUTW, D), BF16),
            vmem((4, 4, PART, D), BF16),
            vmem((4, ROWS, D), BF16),
            vmem((HEADS, ROWS, LANES), BF16),
            vmem((WIDE, D), BF16),
            vmem((D, WIDE), BF16),
            vmem((LANES, ROWS), F32),
            vmem((OUTW, ROWS), F32),
            vmem((WIDE, ROWS), BF16),
            vmem((GROUPS, 4 * ROWS, LANES), BF16),
            vmem((ROWS, 4 * ROWS), BF16),
            vmem((HEADS, ROWS, LANES), F32),
            vmem((GROUPS, ROWS, LANES), F32),
            vmem((GROUPS, ROWS, LANES), F32),
            vmem((4, LANES, ROWS), F32),
            vmem((4, LANES, ROWS), F32),
            vmem((4, OUTW, ROWS), BF16),
            sem((9,)), sem((4,)), sem((4,)), sem((4,)),
            sem((4, 4)), sem((4, 4)), sem((4, 4)), sem((4, 4)),
            sem((4,)), sem((4,)), sem((4,)), sem((4,)),
        ],
        compiler_params=pltpu.CompilerParams(
            collective_id=0, has_side_effects=True, vmem_limit_bytes=58 * 1024 * 1024
        ),
    )(*rest, w_out.T)
    return result.T


def solution(mesh):
    return jax.shard_map(
        on_device,
        mesh=mesh,
        in_specs=(
            P(("sample", "row"), None),
            P("sample", "row", "col"),
            P("sample"),
            P(),
            P(),
            P(),
            P(),
            P(),
            P(),
            P(None, "col"),
        ),
        out_specs=P(("sample", "row"), "col"),
        check_vma=False,
    )
```

```python
import functools
import math

import jax
import jax.numpy as jnp
from jax import lax
from jax.experimental import pallas as pl
from jax.experimental.pallas import tpu as pltpu
from jax.sharding import PartitionSpec as P

D = 384
HEADS = 16
HD = 24
PAD = 32
WIDE = HEADS * PAD
GROUPS = 4
LANES = 128
ROWS = 256
PART = 64
HALVES = 2
OUTW = 96
MESH = pl.DeviceIdType.MESH
F32 = jnp.float32
BF16 = jnp.bfloat16
MASK_HI = 999424.0
MASK_LO = 576.0


def iota(shape, dim):
    return lax.broadcasted_iota(jnp.int32, shape, dim)


def mm(a, b):
    return lax.dot_general(a, b, (((1,), (0,)), ((), ())), preferred_element_type=F32)


def mm_nt(a, b):
    return lax.dot_general(a, b, (((1,), (1,)), ((), ())), preferred_element_type=F32)


def layer_norm(values, gain):
    values = values.astype(F32)
    centered = values - jnp.mean(values, axis=1, keepdims=True)
    var = jnp.mean(centered * centered, axis=1, keepdims=True)
    return (centered * lax.rsqrt(var + 1e-05) * gain).astype(BF16)


def spread_matrix(width):
    src, dst = iota((D, width), 0), iota((D, width), 1)
    hit = (src == (dst // PAD) * HD + dst % PAD) & (dst % PAD < HD)
    return jnp.where(hit, 1.0, 0.0).astype(BF16)


def spread_rows(width, first):
    dst, src = iota((width, D), 0), iota((width, D), 1)
    hit = (src == (dst // PAD + first) * HD + dst % PAD) & (dst % PAD < HD)
    return jnp.where(hit, 1.0, 0.0).astype(BF16)


def kernel(
    single, bias, mask, gain, w_query, q_bias, w_key, w_value, w_gate, w_out, out,
    s_v, n_v, b_v, mask_v, gain_v, qb_v, wq_v, wk_v, wv_v, wg_v, wo_v,
    ybuf, kbuf, qm, wkt, wvp, gate_v, cols_v, kt, vm, p4, mrep, mrun, acc, part, got, gbuf,
    lsem, bsem, zs, zr, ys, yr, xs, xr, ps, pr, gs, gr, ds, dr, fs, fr,
):
    col = lax.axis_index("col")
    row = lax.axis_index("row")
    x, y, z = col, row // 4, row % 4

    def dev(cx, cy, cz):
        return {"row": cy * 4 + cz, "col": cx}

    def rdma(src, dst, ssem, rsem, target):
        return pltpu.make_async_remote_copy(
            src_ref=src, dst_ref=dst, send_sem=ssem, recv_sem=rsem,
            device_id=target, device_id_type=MESH,
        )

    barrier = pltpu.get_barrier_semaphore()
    peers = [dev((x + k) % 4, y, z) for k in (1, 2, 3)]
    peers += [dev(x, (y + k) % 4, z) for k in (1, 2, 3)]
    peers += [dev(x, y, (z + k) % 4) for k in (1, 2, 3)]
    for peer in peers:
        pl.semaphore_signal(barrier, inc=1, device_id=peer, device_id_type=MESH)

    tokens = 4 * ROWS
    loads = [
        (single, s_v), (gain, gain_v), (q_bias, qb_v), (w_query, wq_v), (w_key, wk_v),
        (w_value, wv_v), (w_gate, wg_v), (w_out, wo_v),
        (mask.at[pl.ds(pl.multiple_of(col * tokens, tokens), tokens)], mask_v),
    ]
    loads = [pltpu.make_async_copy(a, b, lsem.at[i]) for i, (a, b) in enumerate(loads)]
    for load in loads:
        load.start()

    def chunk_cols(d):
        return pl.ds(pl.multiple_of(((z + d) % 4) * ROWS, ROWS), ROWS)

    order = (0, 1, 3, 2)

    def bias_load(d):
        return pltpu.make_async_copy(bias.at[:, :, chunk_cols(d)], b_v.at[d], bsem.at[d])

    for load in loads[:2]:
        load.wait()
    gain_row = gain_v[...].reshape(1, D)
    n_v[...] = layer_norm(s_v[...], gain_row)
    pl.semaphore_wait(barrier, len(peers))

    diag = x == y
    mine = pl.ds(pl.multiple_of(x * PART, PART), PART)
    own = n_v.at[mine]

    def zc():
        return rdma(own, ybuf.at[y], zs.at[0], zr.at[0], dev(x, y, (z + 2) % 4))

    def yc(k):
        return rdma(ybuf.at[y], ybuf.at[y], ys.at[k], yr.at[4 - k], dev(x, (y + k) % 4, z))

    def yw(k):
        other = (y + k) % 4
        return rdma(ybuf.at[other], ybuf.at[other], ys.at[k], yr.at[k], dev(x, other, z))

    def xc(k):
        other = (x + k) % 4
        return rdma(ybuf.at[other], kbuf.at[2, mine], xs.at[k], xr.at[4 - k], dev(other, y, z))

    def xw(k):
        other = (x + k) % 4
        where = kbuf.at[2, pl.ds(pl.multiple_of(other * PART, PART), PART)]
        return rdma(where, where, xs.at[k], xr.at[k], dev(other, y, z))

    def half(i):
        return pl.ds(i * (ROWS // HALVES), ROWS // HALVES)

    def direct(i, k):
        return rdma(n_v.at[half(i)], kbuf.at[0, half(i)], ds.at[i, k], dr.at[i], dev(x, (y + k) % 4, z))

    def onward(i, d):
        return rdma(kbuf.at[0, half(i)], kbuf.at[d, half(i)], fs.at[i, d], fr.at[i, d], dev(x, y, (z + 4 - d) % 4))

    def y_send():
        zc().wait_recv()
        for k in (1, 3, 2):
            yc(k).start()

    def x_send():
        for k in (1, 3, 2):
            yw(k).wait_recv()
        for k in (1, 3, 2):
            xc(k).start()

    def x_wait():
        for k in (1, 3, 2):
            xw(k).wait_recv()
        kbuf[2, mine] = ybuf[x]

    def onward_wait(d):
        for i in range(HALVES):
            onward(i, d).wait_recv()

    zc().start()

    @pl.when(diag)
    def _():
        for i in range(HALVES):
            for k in (1, 3, 2):
                direct(i, k).start()
        kbuf[0] = n_v[...]
        for i in range(HALVES):
            for d in (1, 3):
                onward(i, d).start()

    for d in order:
        bias_load(d).start()
    for load in loads[2:]:
        load.wait()

    normed = n_v[...]
    spread = spread_matrix(WIDE)
    spread_t = spread_rows(WIDE, 0)
    wqp = mm(wq_v[...], spread).astype(BF16)
    qb_row = qb_v[...].reshape(1, D)
    qb_hi = qb_row.astype(BF16)
    qb_rest = qb_row - qb_hi.astype(F32)
    qb_mid = qb_rest.astype(BF16)
    qb_lo = (qb_rest - qb_mid.astype(F32)).astype(BF16)
    qb_pad = mm(qb_hi, spread) + mm(qb_mid, spread) + mm(qb_lo, spread)
    query = (mm(normed, wqp) + qb_pad) * (1.0 / math.sqrt(HD))
    wide_lane = iota((ROWS, WIDE), 1) % PAD
    query = jnp.where((wide_lane == HD) | (wide_lane == HD + 1), 1.0, query)
    lane = iota((ROWS, LANES), 1)
    head_of, sub = lane // PAD, lane % PAD
    for h in range(HEADS):
        g, hh = divmod(h, 4)
        qm[h] = jnp.where(head_of == hh, query[:, g * LANES : (g + 1) * LANES], 0.0).astype(BF16)
    wkt[...] = mm_nt(spread_t, wk_v[...]).astype(BF16)
    wvp[...] = mm(wv_v[...], spread).astype(BF16)

    @pl.when(jnp.logical_not(diag))
    def _():
        for i in range(HALVES):
            direct(i, 1).wait_recv()
            for d in (1, 3):
                onward(i, d).start()

    y_send()

    wgt = mm_nt(spread_rows(LANES, col * 4), wg_v[...]).astype(BF16)
    gate_v[...] = jax.nn.sigmoid(mm_nt(wgt, normed))
    pick = iota((OUTW, D), 1) == iota((OUTW, D), 0) + col * OUTW
    cols_v[...] = mm_nt(jnp.where(pick, 1.0, 0.0).astype(BF16), s_v[...])
    mrep[...] = jnp.full(mrep.shape, -1e30, F32)
    mrun[...] = jnp.full(mrun.shape, -1e30, F32)
    acc[...] = jnp.zeros(acc.shape, F32)

    def prepare(d):
        normed_k = kbuf[d]
        keys = mm_nt(wkt[...], normed_k)
        flags = mask_v[chunk_cols(d)].reshape(1, ROWS).astype(F32) - 1.0
        feature = iota((WIDE, ROWS), 0) % PAD
        term = jnp.where(feature == HD, MASK_HI, jnp.where(feature == HD + 1, MASK_LO, 0.0))
        kt[...] = (keys + term * flags).astype(BF16)
        value = mm(normed_k, wvp[...])
        value = jnp.where(wide_lane == HD, 1.0, value)
        for h in range(HEADS):
            g, hh = divmod(h, 4)
            vm[g, hh * ROWS : (hh + 1) * ROWS] = jnp.where(
                head_of == hh, value[:, g * LANES : (g + 1) * LANES], 0.0
            ).astype(BF16)

    def scores(d, g, turn):
        key_tile = kt[g * LANES : (g + 1) * LANES] if isinstance(g, int) else kt[pl.ds(pl.multiple_of(g * LANES, LANES), LANES)]
        old = mrun[g]
        new = old
        for hh in range(4):
            h = g * 4 + hh
            logits = mm(qm[h], key_tile) + b_v[d, h].astype(F32)
            peak = jnp.maximum(jnp.max(logits, axis=1, keepdims=True), mrep[h])
            mrep[h] = peak
            for j in (0, LANES):
                p4[turn, :, hh * ROWS + j : hh * ROWS + j + LANES] = jnp.exp(logits[:, j : j + LANES] - peak).astype(BF16)
            new = jnp.where(head_of == hh, peak, new)
        mrun[g] = new
        acc[g] = acc[g] * jnp.exp(old - new)

    def values(g, turn):
        acc[g] += mm(p4[turn], vm[g])

    def chunk(d, between=None):
        bias_load(d).wait()
        prepare(d)
        for g in range(GROUPS):
            scores(d, g, g % 2)
            if g:
                values(g - 1, (g - 1) % 2)
            if g == 1 and between is not None:
                between()
        values(GROUPS - 1, (GROUPS - 1) % 2)

    chunk(0, x_send)
    onward_wait(1)
    chunk(1)
    onward_wait(3)
    chunk(3)
    x_wait()
    bias_load(2).wait()
    prepare(2)

    def pc(k):
        other = (x + k) % 4
        return rdma(part.at[other], got.at[4 - k], ps.at[k], pr.at[4 - k], dev(other, y, z))

    def pw(k):
        other = (x + k) % 4
        return rdma(got.at[k], got.at[k], ps.at[k], pr.at[k], dev(other, y, z))

    def finish(g):
        whole = jnp.where(sub == HD + 1, mrun[g], acc[g]).T
        heads = [whole[hh * PAD : (hh + 1) * PAD] for hh in range(4)]
        for hh in range(4):
            part[g, hh * HD : (hh + 1) * HD] = heads[hh][0:HD]
        stats = [h[HD : HD + 1] for h in heads] + [h[HD + 1 : HD + 2] for h in heads]
        part[g, OUTW : OUTW + 8] = jnp.concatenate(stats, axis=0)

    def send(k):
        finish((x + k) % 4)
        pc(k).start()

    for k in range(1, 5):
        scores(2, (x + k) % 4, k % 2)
        if k > 1:
            values((x + k - 1) % 4, (k - 1) % 2)
            send(k - 1)
    values(x, 0)
    finish(x)
    for k in (1, 2, 3):
        pw(k).wait_recv()

    parts = [part.at[x]] + [got.at[k] for k in (1, 2, 3)]
    all_sums = [p[0:OUTW] for p in parts]
    all_denoms = [p[OUTW : OUTW + 4] for p in parts]
    all_peaks = [p[OUTW + 4 : OUTW + 8] for p in parts]
    peak = jnp.maximum(jnp.maximum(all_peaks[0], all_peaks[1]), jnp.maximum(all_peaks[2], all_peaks[3]))
    factors = [jnp.exp(p - peak) for p in all_peaks]
    inverse = 1.0 / sum(f * n for f, n in zip(factors, all_denoms))
    factors = [f * inverse for f in factors]
    rows = []
    for hh in range(4):
        inside = slice(hh * HD, (hh + 1) * HD)
        total = sum(s[inside] * f[hh : hh + 1] for s, f in zip(all_sums, factors))
        rows.append(gate_v[hh * PAD : hh * PAD + HD] * total)
    gbuf[x] = jnp.concatenate(rows, axis=0).astype(BF16)

    def gc(k):
        return rdma(gbuf.at[x], gbuf.at[x], gs.at[k], gr.at[4 - k], dev((x + k) % 4, y, z))

    def gw(k):
        other = (x + k) % 4
        return rdma(gbuf.at[other], gbuf.at[other], gs.at[k], gr.at[k], dev(other, y, z))

    for k in (1, 3, 2):
        gc(k).start()
    for k in (1, 3, 2):
        gw(k).wait_recv()
    out[...] = cols_v[...] + mm(wo_v[...], gbuf[...].reshape(D, ROWS))

    zc().wait_send()
    for k in (1, 2, 3):
        yc(k).wait_send()
        xc(k).wait_send()
    for i in range(HALVES):
        for d in (1, 3):
            onward(i, d).wait_send()

    @pl.when(diag)
    def _():
        for i in range(HALVES):
            for k in (1, 2, 3):
                direct(i, k).wait_send()

    for k in (1, 2, 3):
        pc(k).wait_send()
        gc(k).wait_send()


def on_device(*args):
    *rest, w_out = args
    hbm = pl.BlockSpec(memory_space=pltpu.MemorySpace.HBM)
    sem = pltpu.SemaphoreType.DMA
    vmem = pltpu.VMEM
    result = pl.pallas_call(
        kernel,
        name="attention",
        out_shape=jax.ShapeDtypeStruct((OUTW, ROWS), F32),
        in_specs=[hbm] * 10,
        out_specs=pl.BlockSpec(memory_space=pltpu.VMEM),
        scratch_shapes=[
            vmem((ROWS, D), BF16),
            vmem((ROWS, D), BF16),
            vmem((4, HEADS, ROWS, ROWS), BF16),
            vmem((4 * ROWS,), jnp.int32),
            vmem((D,), F32),
            vmem((D,), F32),
            vmem((D, D), BF16),
            vmem((D, D), BF16),
            vmem((D, D), BF16),
            vmem((D, D), BF16),
            vmem((OUTW, D), BF16),
            vmem((4, PART, D), BF16),
            vmem((4, ROWS, D), BF16),
            vmem((HEADS, ROWS, LANES), BF16),
            vmem((WIDE, D), BF16),
            vmem((D, WIDE), BF16),
            vmem((LANES, ROWS), F32),
            vmem((OUTW, ROWS), F32),
            vmem((WIDE, ROWS), BF16),
            vmem((GROUPS, 4 * ROWS, LANES), BF16),
            vmem((2, ROWS, 4 * ROWS), BF16),
            vmem((HEADS, ROWS, LANES), F32),
            vmem((GROUPS, ROWS, LANES), F32),
            vmem((GROUPS, ROWS, LANES), F32),
            vmem((4, OUTW + 8, ROWS), F32),
            vmem((4, OUTW + 8, ROWS), F32),
            vmem((4, OUTW, ROWS), BF16),
            sem((9,)), sem((4,)), sem((1,)), sem((1,)),
            sem((4,)), sem((4,)), sem((4,)), sem((4,)),
            sem((4,)), sem((4,)), sem((4,)), sem((4,)),
            sem((HALVES, 4)), sem((HALVES,)), sem((HALVES, 4)), sem((HALVES, 4)),
        ],
        compiler_params=pltpu.CompilerParams(
            collective_id=0, has_side_effects=True, vmem_limit_bytes=58 * 1024 * 1024
        ),
    )(*rest, w_out.T)
    return result.T


def solution(mesh):
    return jax.shard_map(
        on_device,
        mesh=mesh,
        in_specs=(
            P(("sample", "row"), None),
            P("sample", "row", "col"),
            P("sample"),
            P(),
            P(),
            P(),
            P(),
            P(),
            P(),
            P(None, "col"),
        ),
        out_specs=P(("sample", "row"), "col"),
        check_vma=False,
    )
```

```python
import functools
import math

import jax
import jax.numpy as jnp
from jax import lax
from jax.experimental import pallas as pl
from jax.experimental.pallas import tpu as pltpu
from jax.sharding import PartitionSpec as P

D = 384
HEADS = 16
HD = 24
PAD = 32
WIDE = HEADS * PAD
GROUPS = 4
LANES = 128
ROWS = 256
PART = 64
HALVES = 2
OUTW = 96
MESH = pl.DeviceIdType.MESH
F32 = jnp.float32
BF16 = jnp.bfloat16
MASK_HI = 999424.0
MASK_LO = 576.0


def iota(shape, dim):
    return lax.broadcasted_iota(jnp.int32, shape, dim)


def mm(a, b):
    return lax.dot_general(a, b, (((1,), (0,)), ((), ())), preferred_element_type=F32)


def mm_nt(a, b):
    return lax.dot_general(a, b, (((1,), (1,)), ((), ())), preferred_element_type=F32)


def layer_norm(values, gain):
    values = values.astype(F32)
    centered = values - jnp.mean(values, axis=1, keepdims=True)
    var = jnp.mean(centered * centered, axis=1, keepdims=True)
    return (centered * lax.rsqrt(var + 1e-05) * gain).astype(BF16)


def spread_matrix(width):
    src, dst = iota((D, width), 0), iota((D, width), 1)
    hit = (src == (dst // PAD) * HD + dst % PAD) & (dst % PAD < HD)
    return jnp.where(hit, 1.0, 0.0).astype(BF16)


def spread_rows(width, first):
    dst, src = iota((width, D), 0), iota((width, D), 1)
    hit = (src == (dst // PAD + first) * HD + dst % PAD) & (dst % PAD < HD)
    return jnp.where(hit, 1.0, 0.0).astype(BF16)


def kernel(
    single, bias, mask, gain, w_query, q_bias, w_key, w_value, w_gate, w_out, out,
    s_v, n_v, b_v, mask_v, gain_v, qb_v, wq_v, wk_v, wv_v, wg_v, wo_v,
    ybuf, kbuf, qm, wkt, wvp, gate_v, cols_v, kt, vm, p4, mrep, mrun, acc, part, got, gbuf,
    lsem, bsem, zs, zr, ys, yr, xs, xr, ps, pr, gs, gr, ds, dr, fs, fr,
):
    col = lax.axis_index("col")
    row = lax.axis_index("row")
    x, y, z = col, row // 4, row % 4

    def dev(cx, cy, cz):
        return {"row": cy * 4 + cz, "col": cx}

    def rdma(src, dst, ssem, rsem, target):
        return pltpu.make_async_remote_copy(
            src_ref=src, dst_ref=dst, send_sem=ssem, recv_sem=rsem,
            device_id=target, device_id_type=MESH,
        )

    barrier = pltpu.get_barrier_semaphore()
    peers = [dev((x + k) % 4, y, z) for k in (1, 2, 3)]
    peers += [dev(x, (y + k) % 4, z) for k in (1, 2, 3)]
    peers += [dev(x, y, (z + k) % 4) for k in (1, 2, 3)]
    for peer in peers:
        pl.semaphore_signal(barrier, inc=1, device_id=peer, device_id_type=MESH)

    tokens = 4 * ROWS
    loads = [
        (single, s_v), (gain, gain_v), (q_bias, qb_v), (w_query, wq_v), (w_key, wk_v),
        (w_value, wv_v), (w_gate, wg_v), (w_out, wo_v),
        (mask.at[pl.ds(pl.multiple_of(col * tokens, tokens), tokens)], mask_v),
    ]
    loads = [pltpu.make_async_copy(a, b, lsem.at[i]) for i, (a, b) in enumerate(loads)]
    for load in loads:
        load.start()

    def chunk_cols(d):
        return pl.ds(pl.multiple_of(((z + d) % 4) * ROWS, ROWS), ROWS)

    order = (0, 1, 3, 2)

    def bias_load(d):
        return pltpu.make_async_copy(bias.at[:, :, chunk_cols(d)], b_v.at[d], bsem.at[d])

    for load in loads[:2]:
        load.wait()
    gain_row = gain_v[...].reshape(1, D)
    n_v[...] = layer_norm(s_v[...], gain_row)
    pl.semaphore_wait(barrier, len(peers))

    diag = x == y
    mine = pl.ds(pl.multiple_of(x * PART, PART), PART)
    own = n_v.at[mine]

    def zc():
        return rdma(own, ybuf.at[y], zs.at[0], zr.at[0], dev(x, y, (z + 2) % 4))

    def yc(k):
        return rdma(ybuf.at[y], ybuf.at[y], ys.at[k], yr.at[4 - k], dev(x, (y + k) % 4, z))

    def yw(k):
        other = (y + k) % 4
        return rdma(ybuf.at[other], ybuf.at[other], ys.at[k], yr.at[k], dev(x, other, z))

    def xc(k):
        other = (x + k) % 4
        return rdma(ybuf.at[other], kbuf.at[2, mine], xs.at[k], xr.at[4 - k], dev(other, y, z))

    def xw(k):
        other = (x + k) % 4
        where = kbuf.at[2, pl.ds(pl.multiple_of(other * PART, PART), PART)]
        return rdma(where, where, xs.at[k], xr.at[k], dev(other, y, z))

    def half(i):
        return pl.ds(i * (ROWS // HALVES), ROWS // HALVES)

    def direct(i, k):
        return rdma(n_v.at[half(i)], kbuf.at[0, half(i)], ds.at[i, k], dr.at[i], dev(x, (y + k) % 4, z))

    def onward(i, d):
        return rdma(kbuf.at[0, half(i)], kbuf.at[d, half(i)], fs.at[i, d], fr.at[i, d], dev(x, y, (z + 4 - d) % 4))

    def y_send():
        zc().wait_recv()
        for k in (1, 3, 2):
            yc(k).start()

    def x_send():
        for k in (1, 3, 2):
            yw(k).wait_recv()
        for k in (1, 3, 2):
            xc(k).start()

    def x_wait():
        for k in (1, 3, 2):
            xw(k).wait_recv()
        kbuf[2, mine] = ybuf[x]

    def onward_wait(d):
        for i in range(HALVES):
            onward(i, d).wait_recv()

    zc().start()

    @pl.when(diag)
    def _():
        for i in range(HALVES):
            for k in (1, 3, 2):
                direct(i, k).start()
        kbuf[0] = n_v[...]
        for i in range(HALVES):
            for d in (1, 3):
                onward(i, d).start()

    for d in order:
        bias_load(d).start()
    for load in loads[2:]:
        load.wait()

    normed = n_v[...]
    spread = spread_matrix(WIDE)
    spread_t = spread_rows(WIDE, 0)
    wqp = mm(wq_v[...], spread).astype(BF16)
    qb_row = qb_v[...].reshape(1, D)
    qb_hi = qb_row.astype(BF16)
    qb_rest = qb_row - qb_hi.astype(F32)
    qb_mid = qb_rest.astype(BF16)
    qb_lo = (qb_rest - qb_mid.astype(F32)).astype(BF16)
    qb_pad = mm(qb_hi, spread) + mm(qb_mid, spread) + mm(qb_lo, spread)
    query = (mm(normed, wqp) + qb_pad) * (1.0 / math.sqrt(HD))
    wide_lane = iota((ROWS, WIDE), 1) % PAD
    query = jnp.where((wide_lane == HD) | (wide_lane == HD + 1), 1.0, query)
    lane = iota((ROWS, LANES), 1)
    head_of, sub = lane // PAD, lane % PAD
    for h in range(HEADS):
        g, hh = divmod(h, 4)
        qm[h] = jnp.where(head_of == hh, query[:, g * LANES : (g + 1) * LANES], 0.0).astype(BF16)
    wkt[...] = mm_nt(spread_t, wk_v[...]).astype(BF16)
    wvp[...] = mm(wv_v[...], spread).astype(BF16)

    @pl.when(jnp.logical_not(diag))
    def _():
        for i in range(HALVES):
            direct(i, 1).wait_recv()
            for d in (1, 3):
                onward(i, d).start()

    y_send()

    wgt = mm_nt(spread_rows(LANES, col * 4), wg_v[...]).astype(BF16)
    gate_v[...] = jax.nn.sigmoid(mm_nt(wgt, normed))
    pick = iota((OUTW, D), 1) == iota((OUTW, D), 0) + col * OUTW
    cols_v[...] = mm_nt(jnp.where(pick, 1.0, 0.0).astype(BF16), s_v[...])
    mrep[...] = jnp.full(mrep.shape, -1e30, F32)
    mrun[...] = jnp.full(mrun.shape, -1e30, F32)
    acc[...] = jnp.zeros(acc.shape, F32)

    def prepare(d):
        normed_k = kbuf[d]
        keys = mm_nt(wkt[...], normed_k)
        flags = mask_v[chunk_cols(d)].reshape(1, ROWS).astype(F32) - 1.0
        feature = iota((WIDE, ROWS), 0) % PAD
        term = jnp.where(feature == HD, MASK_HI, jnp.where(feature == HD + 1, MASK_LO, 0.0))
        kt[...] = (keys + term * flags).astype(BF16)
        value = mm(normed_k, wvp[...])
        value = jnp.where(wide_lane == HD, 1.0, value)
        for h in range(HEADS):
            g, hh = divmod(h, 4)
            vm[g, hh * ROWS : (hh + 1) * ROWS] = jnp.where(
                head_of == hh, value[:, g * LANES : (g + 1) * LANES], 0.0
            ).astype(BF16)

    def scores(d, g, turn):
        key_tile = kt[g * LANES : (g + 1) * LANES] if isinstance(g, int) else kt[pl.ds(pl.multiple_of(g * LANES, LANES), LANES)]
        old = mrun[g]
        new = old
        for hh in range(4):
            h = g * 4 + hh
            logits = mm(qm[h], key_tile) + b_v[d, h].astype(F32)
            peak = jnp.maximum(jnp.max(logits, axis=1, keepdims=True), mrep[h])
            mrep[h] = peak
            for j in (0, LANES):
                p4[turn, :, hh * ROWS + j : hh * ROWS + j + LANES] = jnp.exp(logits[:, j : j + LANES] - peak).astype(BF16)
            new = jnp.where(head_of == hh, peak, new)
        mrun[g] = new
        acc[g] = acc[g] * jnp.exp(old - new)

    def values(g, turn):
        acc[g] += mm(p4[turn], vm[g])

    def chunk(d, between=None):
        bias_load(d).wait()
        prepare(d)
        for g in range(GROUPS):
            scores(d, g, g % 2)
            if g:
                values(g - 1, (g - 1) % 2)
            if g == 1 and between is not None:
                between()
        values(GROUPS - 1, (GROUPS - 1) % 2)

    chunk(0, x_send)
    onward_wait(1)
    chunk(1)
    onward_wait(3)
    chunk(3)
    x_wait()
    bias_load(2).wait()
    prepare(2)

    def pc(k):
        other = (x + k) % 4
        return rdma(part.at[other], got.at[4 - k], ps.at[k], pr.at[4 - k], dev(other, y, z))

    def pw(k):
        other = (x + k) % 4
        return rdma(got.at[k], got.at[k], ps.at[k], pr.at[k], dev(other, y, z))

    def finish(g):
        whole = jnp.where(sub == HD + 1, mrun[g], acc[g]).T
        heads = [whole[hh * PAD : (hh + 1) * PAD] for hh in range(4)]
        for hh in range(4):
            part[g, hh * HD : (hh + 1) * HD] = heads[hh][0:HD]
        stats = [h[HD : HD + 1] for h in heads] + [h[HD + 1 : HD + 2] for h in heads]
        part[g, OUTW : OUTW + 8] = jnp.concatenate(stats, axis=0)

    def send(k):
        finish((x + k) % 4)
        pc(k).start()

    turns = (2, 1, 3, 0)
    for i, k in enumerate(turns):
        scores(2, (x + k) % 4, i % 2)
        if i:
            values((x + turns[i - 1]) % 4, (i - 1) % 2)
            send(turns[i - 1])
    values(x, 1)
    finish(x)
    for k in (1, 2, 3):
        pw(k).wait_recv()

    parts = [part.at[x]] + [got.at[k] for k in (1, 2, 3)]
    all_sums = [p[0:OUTW] for p in parts]
    all_denoms = [p[OUTW : OUTW + 4] for p in parts]
    all_peaks = [p[OUTW + 4 : OUTW + 8] for p in parts]
    peak = jnp.maximum(jnp.maximum(all_peaks[0], all_peaks[1]), jnp.maximum(all_peaks[2], all_peaks[3]))
    factors = [jnp.exp(p - peak) for p in all_peaks]
    inverse = 1.0 / sum(f * n for f, n in zip(factors, all_denoms))
    factors = [f * inverse for f in factors]
    rows = []
    for hh in range(4):
        inside = slice(hh * HD, (hh + 1) * HD)
        total = sum(s[inside] * f[hh : hh + 1] for s, f in zip(all_sums, factors))
        rows.append(gate_v[hh * PAD : hh * PAD + HD] * total)
    gbuf[x] = jnp.concatenate(rows, axis=0).astype(BF16)

    def gc(k):
        return rdma(gbuf.at[x], gbuf.at[x], gs.at[k], gr.at[4 - k], dev((x + k) % 4, y, z))

    def gw(k):
        other = (x + k) % 4
        return rdma(gbuf.at[other], gbuf.at[other], gs.at[k], gr.at[k], dev(other, y, z))

    for k in (1, 3, 2):
        gc(k).start()
    for k in (1, 3, 2):
        gw(k).wait_recv()
    out[...] = cols_v[...] + mm(wo_v[...], gbuf[...].reshape(D, ROWS))

    zc().wait_send()
    for k in (1, 2, 3):
        yc(k).wait_send()
        xc(k).wait_send()
    for i in range(HALVES):
        for d in (1, 3):
            onward(i, d).wait_send()

    @pl.when(diag)
    def _():
        for i in range(HALVES):
            for k in (1, 2, 3):
                direct(i, k).wait_send()

    for k in (1, 2, 3):
        pc(k).wait_send()
        gc(k).wait_send()


def on_device(*args):
    *rest, w_out = args
    hbm = pl.BlockSpec(memory_space=pltpu.MemorySpace.HBM)
    sem = pltpu.SemaphoreType.DMA
    vmem = pltpu.VMEM
    result = pl.pallas_call(
        kernel,
        name="attention",
        out_shape=jax.ShapeDtypeStruct((OUTW, ROWS), F32),
        in_specs=[hbm] * 10,
        out_specs=pl.BlockSpec(memory_space=pltpu.VMEM),
        scratch_shapes=[
            vmem((ROWS, D), BF16),
            vmem((ROWS, D), BF16),
            vmem((4, HEADS, ROWS, ROWS), BF16),
            vmem((4 * ROWS,), jnp.int32),
            vmem((D,), F32),
            vmem((D,), F32),
            vmem((D, D), BF16),
            vmem((D, D), BF16),
            vmem((D, D), BF16),
            vmem((D, D), BF16),
            vmem((OUTW, D), BF16),
            vmem((4, PART, D), BF16),
            vmem((4, ROWS, D), BF16),
            vmem((HEADS, ROWS, LANES), BF16),
            vmem((WIDE, D), BF16),
            vmem((D, WIDE), BF16),
            vmem((LANES, ROWS), F32),
            vmem((OUTW, ROWS), F32),
            vmem((WIDE, ROWS), BF16),
            vmem((GROUPS, 4 * ROWS, LANES), BF16),
            vmem((2, ROWS, 4 * ROWS), BF16),
            vmem((HEADS, ROWS, LANES), F32),
            vmem((GROUPS, ROWS, LANES), F32),
            vmem((GROUPS, ROWS, LANES), F32),
            vmem((4, OUTW + 8, ROWS), F32),
            vmem((4, OUTW + 8, ROWS), F32),
            vmem((4, OUTW, ROWS), BF16),
            sem((9,)), sem((4,)), sem((1,)), sem((1,)),
            sem((4,)), sem((4,)), sem((4,)), sem((4,)),
            sem((4,)), sem((4,)), sem((4,)), sem((4,)),
            sem((HALVES, 4)), sem((HALVES,)), sem((HALVES, 4)), sem((HALVES, 4)),
        ],
        compiler_params=pltpu.CompilerParams(
            collective_id=0, has_side_effects=True, vmem_limit_bytes=58 * 1024 * 1024
        ),
    )(*rest, w_out.T)
    return result.T


def solution(mesh):
    return jax.shard_map(
        on_device,
        mesh=mesh,
        in_specs=(
            P(("sample", "row"), None),
            P("sample", "row", "col"),
            P("sample"),
            P(),
            P(),
            P(),
            P(),
            P(),
            P(),
            P(None, "col"),
        ),
        out_specs=P(("sample", "row"), "col"),
        check_vma=False,
    )
```

```python
import functools
import math

import jax
import jax.numpy as jnp
from jax import lax
from jax.experimental import pallas as pl
from jax.experimental.pallas import tpu as pltpu
from jax.sharding import PartitionSpec as P

D = 384
HEADS = 16
HD = 24
PAD = 32
WIDE = HEADS * PAD
GROUPS = 4
LANES = 128
ROWS = 256
PART = 64
HALVES = 2
OUTW = 96
MESH = pl.DeviceIdType.MESH
F32 = jnp.float32
BF16 = jnp.bfloat16
MASK_HI = 999424.0
MASK_LO = 576.0


def iota(shape, dim):
    return lax.broadcasted_iota(jnp.int32, shape, dim)


def mm(a, b):
    return lax.dot_general(a, b, (((1,), (0,)), ((), ())), preferred_element_type=F32)


def mm_nt(a, b):
    return lax.dot_general(a, b, (((1,), (1,)), ((), ())), preferred_element_type=F32)


def layer_norm(values, gain):
    values = values.astype(F32)
    centered = values - jnp.mean(values, axis=1, keepdims=True)
    var = jnp.mean(centered * centered, axis=1, keepdims=True)
    return (centered * lax.rsqrt(var + 1e-05) * gain).astype(BF16)


def spread_matrix(width):
    src, dst = iota((D, width), 0), iota((D, width), 1)
    hit = (src == (dst // PAD) * HD + dst % PAD) & (dst % PAD < HD)
    return jnp.where(hit, 1.0, 0.0).astype(BF16)


def spread_rows(width, first):
    dst, src = iota((width, D), 0), iota((width, D), 1)
    hit = (src == (dst // PAD + first) * HD + dst % PAD) & (dst % PAD < HD)
    return jnp.where(hit, 1.0, 0.0).astype(BF16)


def kernel(
    single, bias, mask, gain, w_query, q_bias, w_key, w_value, w_gate, w_out, out,
    s_v, n_v, b_v, mask_v, gain_v, qb_v, wq_v, wk_v, wv_v, wg_v, wo_v,
    ybuf, kbuf, qm, wkt, wvp, gate_v, cols_v, kt, vm, p4, mrep, mrun, acc, part, got, gbuf,
    lsem, bsem, zs, zr, ys, yr, xs, xr, ps, pr, gs, gr, ds, dr, fs, fr,
):
    col = lax.axis_index("col")
    row = lax.axis_index("row")
    x, y, z = col, row // 4, row % 4

    def dev(cx, cy, cz):
        return {"row": cy * 4 + cz, "col": cx}

    def rdma(src, dst, ssem, rsem, target):
        return pltpu.make_async_remote_copy(
            src_ref=src, dst_ref=dst, send_sem=ssem, recv_sem=rsem,
            device_id=target, device_id_type=MESH,
        )

    barrier = pltpu.get_barrier_semaphore()
    peers = [dev((x + k) % 4, y, z) for k in (1, 2, 3)]
    peers += [dev(x, (y + k) % 4, z) for k in (1, 2, 3)]
    peers += [dev(x, y, (z + k) % 4) for k in (1, 2, 3)]
    for peer in peers:
        pl.semaphore_signal(barrier, inc=1, device_id=peer, device_id_type=MESH)

    tokens = 4 * ROWS
    loads = [
        (single, s_v), (gain, gain_v), (q_bias, qb_v), (w_query, wq_v), (w_key, wk_v),
        (w_value, wv_v), (w_gate, wg_v), (w_out, wo_v),
        (mask.at[pl.ds(pl.multiple_of(col * tokens, tokens), tokens)], mask_v),
    ]
    loads = [pltpu.make_async_copy(a, b, lsem.at[i]) for i, (a, b) in enumerate(loads)]
    for load in loads:
        load.start()

    def chunk_cols(d):
        return pl.ds(pl.multiple_of(((z + d) % 4) * ROWS, ROWS), ROWS)

    order = (0, 1, 3, 2)

    def bias_load(d):
        return pltpu.make_async_copy(bias.at[:, :, chunk_cols(d)], b_v.at[d], bsem.at[d])

    for load in loads[:2]:
        load.wait()
    gain_row = gain_v[...].reshape(1, D)
    n_v[...] = layer_norm(s_v[...], gain_row)
    pl.semaphore_wait(barrier, len(peers))

    diag = x == y
    mine = pl.ds(pl.multiple_of(x * PART, PART), PART)
    own = n_v.at[mine]

    def zc():
        return rdma(own, ybuf.at[y], zs.at[0], zr.at[0], dev(x, y, (z + 2) % 4))

    def yc(k):
        return rdma(ybuf.at[y], ybuf.at[y], ys.at[k], yr.at[4 - k], dev(x, (y + k) % 4, z))

    def yw(k):
        other = (y + k) % 4
        return rdma(ybuf.at[other], ybuf.at[other], ys.at[k], yr.at[k], dev(x, other, z))

    def xc(k):
        other = (x + k) % 4
        return rdma(ybuf.at[other], kbuf.at[2, mine], xs.at[k], xr.at[4 - k], dev(other, y, z))

    def xw(k):
        other = (x + k) % 4
        where = kbuf.at[2, pl.ds(pl.multiple_of(other * PART, PART), PART)]
        return rdma(where, where, xs.at[k], xr.at[k], dev(other, y, z))

    def half(i):
        return pl.ds(i * (ROWS // HALVES), ROWS // HALVES)

    def direct(i, k):
        return rdma(n_v.at[half(i)], kbuf.at[0, half(i)], ds.at[i, k], dr.at[i], dev(x, (y + k) % 4, z))

    def onward(i, d):
        return rdma(kbuf.at[0, half(i)], kbuf.at[d, half(i)], fs.at[i, d], fr.at[i, d], dev(x, y, (z + 4 - d) % 4))

    def y_send():
        zc().wait_recv()
        for k in (1, 3, 2):
            yc(k).start()

    def x_send():
        for k in (1, 3, 2):
            yw(k).wait_recv()
        for k in (1, 3, 2):
            xc(k).start()

    def x_wait():
        for k in (1, 3, 2):
            xw(k).wait_recv()
        kbuf[2, mine] = ybuf[x]

    def onward_wait(d):
        for i in range(HALVES):
            onward(i, d).wait_recv()

    zc().start()

    @pl.when(diag)
    def _():
        for i in range(HALVES):
            for k in (1, 3, 2):
                direct(i, k).start()
        kbuf[0] = n_v[...]
        for i in range(HALVES):
            for d in (1, 3):
                onward(i, d).start()

    for d in order:
        bias_load(d).start()
    for load in loads[2:]:
        load.wait()

    normed = n_v[...]
    spread = spread_matrix(WIDE)
    spread_t = spread_rows(WIDE, 0)
    wqp = mm(wq_v[...], spread).astype(BF16)
    qb_row = qb_v[...].reshape(1, D)
    qb_hi = qb_row.astype(BF16)
    qb_rest = qb_row - qb_hi.astype(F32)
    qb_mid = qb_rest.astype(BF16)
    qb_lo = (qb_rest - qb_mid.astype(F32)).astype(BF16)
    qb_pad = mm(qb_hi, spread) + mm(qb_mid, spread) + mm(qb_lo, spread)
    query = (mm(normed, wqp) + qb_pad) * (1.0 / math.sqrt(HD))
    wide_lane = iota((ROWS, WIDE), 1) % PAD
    query = jnp.where((wide_lane == HD) | (wide_lane == HD + 1), 1.0, query)
    lane = iota((ROWS, LANES), 1)
    head_of, sub = lane // PAD, lane % PAD
    for h in range(HEADS):
        g, hh = divmod(h, 4)
        qm[h] = jnp.where(head_of == hh, query[:, g * LANES : (g + 1) * LANES], 0.0).astype(BF16)
    wkt[...] = mm_nt(spread_t, wk_v[...]).astype(BF16)
    wvp[...] = mm(wv_v[...], spread).astype(BF16)

    @pl.when(jnp.logical_not(diag))
    def _():
        for i in range(HALVES):
            direct(i, 1).wait_recv()
            for d in (1, 3):
                onward(i, d).start()

    y_send()

    wgt = mm_nt(spread_rows(LANES, col * 4), wg_v[...]).astype(BF16)
    gate_v[...] = jax.nn.sigmoid(mm_nt(wgt, normed))
    pick = iota((OUTW, D), 1) == iota((OUTW, D), 0) + col * OUTW
    cols_v[...] = mm_nt(jnp.where(pick, 1.0, 0.0).astype(BF16), s_v[...])
    mrep[...] = jnp.full(mrep.shape, -1e30, F32)
    mrun[...] = jnp.full(mrun.shape, -1e30, F32)
    acc[...] = jnp.zeros(acc.shape, F32)

    def prepare(d):
        normed_k = kbuf[d]
        keys = mm_nt(wkt[...], normed_k)
        flags = mask_v[chunk_cols(d)].reshape(1, ROWS).astype(F32) - 1.0
        feature = iota((WIDE, ROWS), 0) % PAD
        term = jnp.where(feature == HD, MASK_HI, jnp.where(feature == HD + 1, MASK_LO, 0.0))
        kt[...] = (keys + term * flags).astype(BF16)
        value = mm(normed_k, wvp[...])
        value = jnp.where(wide_lane == HD, 1.0, value)
        for h in range(HEADS):
            g, hh = divmod(h, 4)
            vm[g, hh * ROWS : (hh + 1) * ROWS] = jnp.where(
                head_of == hh, value[:, g * LANES : (g + 1) * LANES], 0.0
            ).astype(BF16)

    def scores(d, g, turn):
        key_tile = kt[g * LANES : (g + 1) * LANES] if isinstance(g, int) else kt[pl.ds(pl.multiple_of(g * LANES, LANES), LANES)]
        old = mrun[g]
        new = old
        for hh in range(4):
            h = g * 4 + hh
            logits = mm(qm[h], key_tile) + b_v[d, h].astype(F32)
            peak = jnp.maximum(jnp.max(logits, axis=1, keepdims=True), mrep[h])
            mrep[h] = peak
            for j in (0, LANES):
                p4[turn, :, hh * ROWS + j : hh * ROWS + j + LANES] = jnp.exp(logits[:, j : j + LANES] - peak).astype(BF16)
            new = jnp.where(head_of == hh, peak, new)
        mrun[g] = new
        acc[g] = acc[g] * jnp.exp(old - new)

    def values(g, turn):
        acc[g] += mm(p4[turn], vm[g])

    def chunk(d, between=None):
        bias_load(d).wait()
        prepare(d)
        for g in range(GROUPS):
            scores(d, g, g % 2)
            if g:
                values(g - 1, (g - 1) % 2)
            if g == 1 and between is not None:
                between()
        values(GROUPS - 1, (GROUPS - 1) % 2)

    chunk(0, x_send)
    onward_wait(1)
    chunk(1)
    onward_wait(3)
    chunk(3)
    x_wait()
    bias_load(2).wait()
    prepare(2)

    def pc(k):
        other = (x + k) % 4
        return rdma(part.at[other], got.at[4 - k], ps.at[k], pr.at[4 - k], dev(other, y, z))

    def pw(k):
        other = (x + k) % 4
        return rdma(got.at[k], got.at[k], ps.at[k], pr.at[k], dev(other, y, z))

    def finish(g):
        whole = jnp.where(sub == HD + 1, mrun[g], acc[g]).T
        heads = [whole[hh * PAD : (hh + 1) * PAD] for hh in range(4)]
        for hh in range(4):
            part[g, hh * HD : (hh + 1) * HD] = heads[hh][0:HD]
        stats = [h[HD : HD + 1] for h in heads] + [h[HD + 1 : HD + 2] for h in heads]
        part[g, OUTW : OUTW + 8] = jnp.concatenate(stats, axis=0)

    def send(k):
        finish((x + k) % 4)
        pc(k).start()

    turns = (2, 1, 3, 0)
    for i, k in enumerate(turns):
        scores(2, (x + k) % 4, i % 2)
        if i:
            values((x + turns[i - 1]) % 4, (i - 1) % 2)
            send(turns[i - 1])
    values(x, 1)
    finish(x)
    for k in (1, 2, 3):
        pw(k).wait_recv()

    parts = [part.at[x]] + [got.at[k] for k in (1, 2, 3)]
    all_sums = [p[0:OUTW] for p in parts]
    all_denoms = [p[OUTW : OUTW + 4] for p in parts]
    all_peaks = [p[OUTW + 4 : OUTW + 8] for p in parts]
    peak = jnp.maximum(jnp.maximum(all_peaks[0], all_peaks[1]), jnp.maximum(all_peaks[2], all_peaks[3]))
    factors = [jnp.exp(p - peak) for p in all_peaks]
    inverse = 1.0 / sum(f * n for f, n in zip(factors, all_denoms))
    factors = [f * inverse for f in factors]
    rows = []
    for hh in range(4):
        inside = slice(hh * HD, (hh + 1) * HD)
        total = sum(s[inside] * f[hh : hh + 1] for s, f in zip(all_sums, factors))
        rows.append(gate_v[hh * PAD : hh * PAD + HD] * total)
    gbuf[x] = jnp.concatenate(rows, axis=0).astype(BF16)

    def gc(k):
        return rdma(gbuf.at[x], gbuf.at[x], gs.at[k], gr.at[4 - k], dev((x + k) % 4, y, z))

    def gw(k):
        other = (x + k) % 4
        return rdma(gbuf.at[other], gbuf.at[other], gs.at[k], gr.at[k], dev(other, y, z))

    for k in (2, 1, 3):
        gc(k).start()
    for k in (1, 3, 2):
        gw(k).wait_recv()
    out[...] = cols_v[...] + mm(wo_v[...], gbuf[...].reshape(D, ROWS))

    zc().wait_send()
    for k in (1, 2, 3):
        yc(k).wait_send()
        xc(k).wait_send()
    for i in range(HALVES):
        for d in (1, 3):
            onward(i, d).wait_send()

    @pl.when(diag)
    def _():
        for i in range(HALVES):
            for k in (1, 2, 3):
                direct(i, k).wait_send()

    for k in (1, 2, 3):
        pc(k).wait_send()
        gc(k).wait_send()


def on_device(*args):
    *rest, w_out = args
    hbm = pl.BlockSpec(memory_space=pltpu.MemorySpace.HBM)
    sem = pltpu.SemaphoreType.DMA
    vmem = pltpu.VMEM
    result = pl.pallas_call(
        kernel,
        name="attention",
        out_shape=jax.ShapeDtypeStruct((OUTW, ROWS), F32),
        in_specs=[hbm] * 10,
        out_specs=pl.BlockSpec(memory_space=pltpu.VMEM),
        scratch_shapes=[
            vmem((ROWS, D), BF16),
            vmem((ROWS, D), BF16),
            vmem((4, HEADS, ROWS, ROWS), BF16),
            vmem((4 * ROWS,), jnp.int32),
            vmem((D,), F32),
            vmem((D,), F32),
            vmem((D, D), BF16),
            vmem((D, D), BF16),
            vmem((D, D), BF16),
            vmem((D, D), BF16),
            vmem((OUTW, D), BF16),
            vmem((4, PART, D), BF16),
            vmem((4, ROWS, D), BF16),
            vmem((HEADS, ROWS, LANES), BF16),
            vmem((WIDE, D), BF16),
            vmem((D, WIDE), BF16),
            vmem((LANES, ROWS), F32),
            vmem((OUTW, ROWS), F32),
            vmem((WIDE, ROWS), BF16),
            vmem((GROUPS, 4 * ROWS, LANES), BF16),
            vmem((2, ROWS, 4 * ROWS), BF16),
            vmem((HEADS, ROWS, LANES), F32),
            vmem((GROUPS, ROWS, LANES), F32),
            vmem((GROUPS, ROWS, LANES), F32),
            vmem((4, OUTW + 8, ROWS), F32),
            vmem((4, OUTW + 8, ROWS), F32),
            vmem((4, OUTW, ROWS), BF16),
            sem((9,)), sem((4,)), sem((1,)), sem((1,)),
            sem((4,)), sem((4,)), sem((4,)), sem((4,)),
            sem((4,)), sem((4,)), sem((4,)), sem((4,)),
            sem((HALVES, 4)), sem((HALVES,)), sem((HALVES, 4)), sem((HALVES, 4)),
        ],
        compiler_params=pltpu.CompilerParams(
            collective_id=0, has_side_effects=True, vmem_limit_bytes=58 * 1024 * 1024
        ),
    )(*rest, w_out.T)
    return result.T


def solution(mesh):
    return jax.shard_map(
        on_device,
        mesh=mesh,
        in_specs=(
            P(("sample", "row"), None),
            P("sample", "row", "col"),
            P("sample"),
            P(),
            P(),
            P(),
            P(),
            P(),
            P(),
            P(None, "col"),
        ),
        out_specs=P(("sample", "row"), "col"),
        check_vma=False,
    )
```
